256 devices in a mesh: dp: 32 (over z, y_hi, core), mp: 8 (over x, y_lo).
Axes of the slice: x: 4, y: 4 (y_hi: 2, y_lo: 2; y = y_hi * 2 + y_lo), z: 8, core: 2. Of those that a mesh axis runs over, the one named last changes fastest.
Arguments:
- queries: bfloat16 [512, 4, 12288], P('dp', None, 'mp'), may hold values from -14 to 14
- new_keys: bfloat16 [512, 4, 1024], P('dp', None, 'mp'), may hold values from -13 to 13
- new_values: bfloat16 [512, 4, 1024], P('dp', None, 'mp'), may hold values from -24 to 24
- key_cache: bfloat16 [512, 8, 128, 128], P('dp', 'mp'), may hold values from -13 to 13
- value_cache: bfloat16 [512, 8, 128, 128], P('dp', 'mp'), may hold values from -24 to 24
- key_spill: bfloat16 [512, 8, 128, 128], P('dp', 'mp'), may hold values from -13 to 13
- value_spill: bfloat16 [512, 8, 128, 128], P('dp', 'mp'), may hold values from -24 to 24
- lengths: int32 [512], replicated, may hold values from 2 to 256, as said below
- partner: int32 [32], replicated, may hold values from 0 to 31, as said below
- out_weight: bfloat16 [12288, 12288], P('mp', 'dp'), may hold values from -0.0546875 to 0.0546875
Outputs:
- attention_out: bfloat16 [2048, 12288], P('mp', 'dp')
The draws below stay inside these ranges and needn't reach their ends.
Inputs may be any that keep to these rules, and one draw needn't show every extreme that they name: partner[i] = i XOR 2**b for a single b of 0 to log2(32) - 1 chosen by the draw, so partner pairs the indices of dp and has no fixed point. `lengths`: some row has exactly 256 positions in every draw; the mean length differs from one index of dp to another.
All inputs are finite; a program needn't handle non-finite values.
Results may differ from the reference program's by a relative error of at most 0.0053.
Values may be sent and summed in bfloat16 or wider, within the bound.
A program may use at most 64 MiB of HBM per device.

```python
import math
import jax
import jax.numpy as jnp
from jax import lax

D = 12288
QH = 96
KVH = 8
HD = 128
ROWS_DEV = 16
CAP = 128
S = 4
ROWS_ALL = 512
N_DP = 32


def draw_queries(key, part):
    key = jax.random.fold_in(key, 11)
    first_key = jax.random.fold_in(key, 0)
    values = jnp.clip(jax.random.normal(first_key, (ROWS_ALL, S, QH, HD), jnp.float32), -6.0, 6.0)
    return values.reshape(ROWS_ALL, S, QH * HD).astype(jnp.bfloat16)


def draw_new_keys(key, part):
    key = jax.random.fold_in(key, 17)
    values = jnp.clip(jax.random.normal(key, (ROWS_ALL, S, KVH, HD), jnp.float32), -6.0, 6.0)
    return values.reshape(ROWS_ALL, S, KVH * HD).astype(jnp.bfloat16)


def draw_key_cache(key, part):
    key = jax.random.fold_in(key, 23)
    values = jnp.clip(jax.random.normal(key, (ROWS_ALL, KVH, CAP, HD), jnp.float32), -6.0, 6.0)
    return values.astype(jnp.bfloat16)


def draw_key_spill(key, part):
    key = jax.random.fold_in(key, 29)
    values = jnp.clip(jax.random.normal(key, (ROWS_ALL, KVH, CAP, HD), jnp.float32), -6.0, 6.0)
    return values.astype(jnp.bfloat16)


def draw_lengths(key, part):
    key = jax.random.fold_in(key, 41)
    heavy_key, length_key, peak_key = jax.random.split(key, 3)
    heaviness = jax.random.randint(heavy_key, (N_DP,), 1, 5)
    ceiling = 2 + (2 * CAP - 2) * heaviness // 4
    per_row = jnp.repeat(ceiling, ROWS_DEV)
    drawn_lengths = jax.random.randint(length_key, (ROWS_ALL,), 2, per_row + 1)
    longest = jax.random.randint(peak_key, (), 0, ROWS_ALL)
    return drawn_lengths.at[longest].set(2 * CAP).astype(jnp.int32)


def draw_partner(key, part):
    key = jax.random.fold_in(key, 53)
    level_total = int(math.log2(N_DP))
    which_bit = jax.random.randint(key, (), 0, level_total).astype(jnp.int32)
    offset = jnp.left_shift(jnp.int32(1), which_bit)
    return jnp.bitwise_xor(jnp.arange(N_DP, dtype=jnp.int32), offset)


def level_of(rng, dims, cuts, smallest, top_value):
    def one(axis_at, shards_of):
        draws = jax.random.uniform(jax.random.fold_in(jax.random.fold_in(rng, 6), axis_at), (shards_of,), jnp.float32, smallest / len(cuts), top_value / len(cuts))
        return jnp.repeat(jnp.exp(draws), dims[axis_at] // shards_of).reshape((-1,) + (1,) * (len(dims) - axis_at - 1))

    level = one(*cuts[0])
    for cut in cuts[1:]:
        level = level * one(*cut)
    return level


def normal_values(rng, dims, scale, most, cuts=(), held_as=jnp.bfloat16):
    drawn = jax.random.normal(rng, dims, jnp.float32) * scale
    if len(cuts) > 0:
        drawn = level_of(rng, dims, cuts, -0.22, 0.18) * drawn
    return jnp.clip(drawn, min=-most, max=most).astype(held_as)


def setup_inputs(seed: int = 0) -> dict:
    key_of = jax.random.split(jax.random.key(seed), 11)
    return {
        "queries": draw_queries(jax.random.fold_in(key_of[10], 71), 0),
        "new_keys": draw_new_keys(jax.random.fold_in(key_of[10], 71), 0),
        "new_values": normal_values(key_of[2], (ROWS_ALL, S, KVH * HD), 4.0, 24.0, ((0, 32), (2, 8))),
        "key_cache": draw_key_cache(jax.random.fold_in(key_of[10], 71), 0),
        "value_cache": normal_values(key_of[4], (ROWS_ALL, KVH, CAP, HD), 4.0, 24.0, ((0, 32), (1, 8))),
        "key_spill": draw_key_spill(jax.random.fold_in(key_of[10], 71), 0),
        "value_spill": normal_values(key_of[6], (ROWS_ALL, KVH, CAP, HD), 4.0, 24.0, ((0, 32), (1, 8))),
        "lengths": draw_lengths(jax.random.fold_in(key_of[10], 71), 0),
        "partner": draw_partner(jax.random.fold_in(key_of[10], 71), 0),
        "out_weight": normal_values(key_of[9], (QH * HD, D), (QH * HD) ** -0.5, 0.0546875, ((0, 8), (1, 32))),
    }


MASKED_SCORE = -1e+30

def attend_piece(query_heads, keys, values, valid):
    scaling = 1.0 / math.sqrt(keys.shape[-1])
    scores = jnp.einsum('rskgd,rkcd->rkgsc', query_heads.astype(jnp.float32), keys.astype(jnp.float32)) * scaling
    allowed = valid[:, None, None, :, :]
    masked = jnp.where(allowed, scores, MASKED_SCORE)
    peak_score = lax.optimization_barrier(jnp.max(masked, axis=-1))
    weights = jnp.where(allowed, jnp.exp(masked - peak_score[..., None]), 0.0)
    weight_sum = lax.optimization_barrier(jnp.sum(weights, axis=-1))
    rounded = weights.astype(jnp.bfloat16)
    summed = jnp.einsum('rkgsc,rkcd->rkgsd', rounded.astype(jnp.float32), values.astype(jnp.float32))
    return (peak_score, weight_sum, summed)

def merge_parts(pieces):
    overall_peak = pieces[0][0]
    for entry in pieces[1:]:
        overall_peak = jnp.maximum(overall_peak, entry[0])
    numerator = jnp.zeros_like(pieces[0][2])
    denominator = jnp.zeros_like(pieces[0][1])
    for peak_score, weight_sum, summed in pieces:
        factor = jnp.exp(peak_score - overall_peak)
        numerator = numerator + factor[..., None] * summed
        denominator = denominator + factor * weight_sum
    return numerator / denominator[..., None]

def reference(queries, new_keys, new_values, key_cache, value_cache, key_spill, value_spill, lengths, partner, out_weight):
    group_size = QH // KVH
    step_index = jnp.arange(S, dtype=jnp.int32)
    causal = step_index[None, :] <= step_index[:, None]
    positions = jnp.arange(CAP, dtype=jnp.int32)

    def one_row(row_index):
        device_index = row_index // ROWS_DEV
        tail_row = partner[device_index] * ROWS_DEV + row_index % ROWS_DEV
        length = lengths[row_index]
        query_heads = queries[row_index].reshape(1, S, KVH, group_size, HD)
        own_valid = jnp.broadcast_to((positions < length)[None, None, :], (1, S, CAP))
        tail_valid = jnp.broadcast_to((positions < length - CAP)[None, None, :], (1, S, CAP))
        fresh_keys = new_keys[row_index].reshape(S, KVH, HD).transpose(1, 0, 2)[None]
        fresh_values = new_values[row_index].reshape(S, KVH, HD).transpose(1, 0, 2)[None]
        pieces = [attend_piece(query_heads, key_cache[row_index][None], value_cache[row_index][None], own_valid), attend_piece(query_heads, key_spill[tail_row][None], value_spill[tail_row][None], tail_valid), attend_piece(query_heads, fresh_keys, fresh_values, causal[None])]
        blended = merge_parts(pieces)
        return blended[0].transpose(2, 0, 1, 3).reshape(S, QH * HD).astype(jnp.bfloat16)
    context = lax.map(one_row, jnp.arange(ROWS_ALL, dtype=jnp.int32))
    flattened = context.reshape(ROWS_ALL * S, QH * HD)
    return jnp.dot(flattened, out_weight, preferred_element_type=jnp.float32).astype(jnp.bfloat16)
```

```python
import functools
import math

import jax
import jax.numpy as jnp
from jax import lax
from jax.experimental import pallas as pl
from jax.experimental.pallas import tpu as pltpu
from jax.sharding import PartitionSpec as P

MESH = pl.DeviceIdType.MESH
MASKED = -1e30
F32, BF16 = jnp.float32, jnp.bfloat16

ROWS = 16
STEPS = 4
GROUP = 12
HEAD = 128
CAP = 128
COLS = GROUP * HEAD
OUT_COLS = 384
ROUNDS = 4
RPR = ROWS // ROUNDS
RB = RPR * STEPS
QR = GROUP * STEPS
QB = RPR * QR
Z, MP = 8, 8
SCALE2 = math.log2(math.e) / math.sqrt(HEAD)


def head_major(index):
    head, row, step = index >> 4, (index >> 2) & 3, index & 3
    return row * QR + head * STEPS + step


def kernel(
    bit,
    lengths, q_in, nk, nv, k_hbm, v_hbm, sk_hbm, sv_hbm, w_hbm,
    out,
    k, v, sk, sv, w, q_own, q_far, o_own, m_own, l_own,
    t_send, st_send, t_recv, st_recv, g, ps, pr,
    load_sem, q_ss, q_rs, t_ss, t_rs, st_ss, st_rs, z_ss, y_ss, c_ss, g_rs, p_ss, p_rs,
):
    me, mp = lax.axis_index("dp"), lax.axis_index("mp")
    z, yh, c = me // 4, (me // 2) % 2, me % 2
    mask = 2**bit
    partner = me + mask * (1 - 2 * ((me // mask) % 2))

    def at(zz, yy, cc):
        return {"dp": zz * 4 + yy * 2 + cc, "mp": mp}

    up, down = lax.rem(z + 1, Z), lax.rem(z + Z - 1, Z)
    far = {"dp": partner, "mp": mp}
    near = [at(up, yh, c), at(down, yh, c), at(z, 1 - yh, c), at(z, yh, 1 - c)]

    loads = [
        pltpu.make_async_copy(src, dst, load_sem.at[i])
        for i, (src, dst) in enumerate(
            [(k_hbm, k), (v_hbm, v), (sk_hbm, sk), (sv_hbm, sv), (w_hbm, w)]
        )
    ]
    for load in loads:
        load.start()

    row_id = lax.broadcasted_iota(jnp.int32, (QB, QB), 0)
    col_id = lax.broadcasted_iota(jnp.int32, (QB, QB), 1)
    to_rows = jnp.where(row_id == head_major(col_id), 1.0, 0.0).astype(BF16)
    to_heads = jnp.where(col_id == head_major(row_id), 1.0, 0.0).astype(BF16)
    for s in range(ROUNDS):
        rows = pl.ds(s * RB, RB)
        stacked = jnp.concatenate(
            [q_in[rows, h * HEAD : (h + 1) * HEAD] for h in range(GROUP)], axis=0
        )
        q_own[s] = jnp.dot(to_rows, stacked, preferred_element_type=F32).astype(BF16)

    barrier = pltpu.get_barrier_semaphore()
    for device in near + [far]:
        pl.semaphore_signal(barrier, inc=1, device_id=device, device_id_type=MESH)
    for j in range(1, MP):
        pl.semaphore_signal(
            barrier, inc=1, device_id={"dp": me, "mp": lax.rem(mp + j, MP)}, device_id_type=MESH
        )
    pl.semaphore_wait(barrier, len(near) + 1 + MP - 1)

    def remote(src, dst, send_sem, recv_sem, device):
        return pltpu.make_async_remote_copy(
            src_ref=src, dst_ref=dst, send_sem=send_sem, recv_sem=recv_sem,
            device_id=device, device_id_type=MESH,
        )

    def q_copy(s):
        return remote(q_own.at[s], q_far.at[s], q_ss.at[s], q_rs.at[s], far)

    def t_copy(s):
        return remote(t_send.at[s], t_recv.at[s], t_ss.at[s], t_rs.at[s], far)

    def st_copy(s):
        return remote(st_send.at[s], st_recv.at[s], st_ss.at[s], st_rs.at[s], far)

    for s in range(ROUNDS):
        q_copy(s).start()

    lane = lax.broadcasted_iota(jnp.int32, (1, CAP), 1)

    def bias_of(owner, s, less):
        return jnp.stack(
            [
                jnp.where(lane < lengths[owner * ROWS + s * RPR + r] - less, 0.0, MASKED)
                for r in range(RPR)
            ]
        )

    def scores_of(queries, keys, bias):
        raw = jnp.einsum("rqd,rkd->rqk", queries, keys, preferred_element_type=F32)
        return raw * SCALE2 + bias

    q_row = lax.broadcasted_iota(jnp.int32, (QB, RB), 0)
    f_col = lax.broadcasted_iota(jnp.int32, (QB, RB), 1)
    first = (f_col >> 2) * QR
    fresh_ok = (q_row >= first) & (q_row < first + QR) & ((f_col & 3) <= (q_row & 3))
    fresh_bias = jnp.where(fresh_ok, 0.0, MASKED)
    loads[0].wait()
    loads[1].wait()
    for s in range(ROUNDS):
        rows = pl.ds(s * RPR, RPR)
        queries = q_own[s]
        own = scores_of(queries.reshape(RPR, QR, HEAD), k[rows], bias_of(me, s, 0))
        fresh_keys, fresh_values = nk[pl.ds(s * RB, RB), :], nv[pl.ds(s * RB, RB), :]
        fresh = (
            lax.dot_general(
                queries, fresh_keys, (((1,), (1,)), ((), ())), preferred_element_type=F32
            )
            * SCALE2
            + fresh_bias
        ).reshape(RPR, QR, RB)
        peak = jnp.maximum(
            jnp.max(own, axis=-1, keepdims=True), jnp.max(fresh, axis=-1, keepdims=True)
        )
        own, fresh = jnp.exp2(own - peak), jnp.exp2(fresh - peak)
        m_own[s] = peak
        l_own[s] = jnp.sum(own, axis=-1, keepdims=True) + jnp.sum(fresh, axis=-1, keepdims=True)
        summed = jnp.einsum("rqk,rkd->rqd", own.astype(BF16), v[rows], preferred_element_type=F32)
        o_own[s] = summed + jnp.dot(
            fresh.astype(BF16).reshape(QB, RB), fresh_values, preferred_element_type=F32
        ).reshape(RPR, QR, HEAD)

    diagonal = lax.broadcasted_iota(jnp.int32, (RPR, QR, CAP), 1) == lax.broadcasted_iota(
        jnp.int32, (RPR, QR, CAP), 2
    )
    loads[2].wait()
    loads[3].wait()
    for s in range(ROUNDS):
        rows = pl.ds(s * RPR, RPR)
        bias = bias_of(partner, s, CAP)
        q_copy(s).wait_recv()
        tail = scores_of(q_far[s].reshape(RPR, QR, HEAD), sk[rows], bias)
        peak = jnp.max(tail, axis=-1, keepdims=True)
        tail = jnp.exp2(tail - peak)
        weight = jnp.sum(tail, axis=-1, keepdims=True)
        summed = jnp.einsum("rqk,rkd->rqd", tail.astype(BF16), sv[rows], preferred_element_type=F32)
        t_send[s] = (summed / weight).astype(BF16).reshape(QB, HEAD)
        t_copy(s).start()
        st_send[s, 0:RPR] = jnp.sum(jnp.where(diagonal, peak + jnp.log2(weight), 0.0), axis=1)
        st_copy(s).start()

    def block(s, zz, yy, cc):
        return g.at[s, zz, yy, cc], g_rs.at[s, zz, yy, cc]

    def send(s, zz, yy, cc, sem, device):
        ref, recv = block(s, zz, yy, cc)
        return remote(ref, ref, sem, recv, device)

    def arrived(s, zz, yy, cc):
        send(s, zz, yy, cc, z_ss.at[0, 0, 0, 0], near[0]).wait_recv()

    sent = []

    def forward(s, zz, yy, to):
        for where in to:
            if where in ("up", "down"):
                sem = z_ss.at[s, "up down".split().index(where), zz, yy]
                copy = send(s, zz, yy, c, sem, near[0 if where == "up" else 1])
            elif where == "y":
                copy = send(s, zz, yy, c, y_ss.at[s, zz, yy], near[2])
            else:
                copy = send(s, zz, yy, c, c_ss.at[s, zz, yy], near[3])
            copy.start()
            sent.append(copy)

    def merge(s):
        t_copy(s).wait_recv()
        st_copy(s).wait_recv()
        log_sum = jnp.sum(
            jnp.where(diagonal, st_recv[s, 0:RPR][:, None, :], 0.0), axis=-1, keepdims=True
        )
        peak = jnp.maximum(m_own[s], log_sum)
        near_factor, far_factor = jnp.exp2(m_own[s] - peak), jnp.exp2(log_sum - peak)
        tail = t_recv[s].reshape(RPR, QR, HEAD).astype(F32)
        total = near_factor * o_own[s] + far_factor * tail
        context = (total / (near_factor * l_own[s] + far_factor)).astype(BF16)
        heads = jnp.dot(to_heads, context.reshape(QB, HEAD), preferred_element_type=F32)
        heads = heads.astype(BF16)
        for h in range(GROUP):
            g[s, z, yh, c, :, h * HEAD : (h + 1) * HEAD] = heads[h * RB : (h + 1) * RB]
        forward(s, z, yh, ("up", "down", "y", "core"))

    def plane(d):
        return lax.rem(z + d + Z, Z)

    def ring(s, d):
        if d == 0:
            arrived(s, z, 1 - yh, c)
            forward(s, z, 1 - yh, ("up", "down", "core"))
        elif d < 4:
            below, above = plane(-d), plane(d)
            for which, yy in enumerate((yh, 1 - yh)):
                arrived(s, below, yy, c)
                forward(s, below, yy, ("up", "core") if d < 3 or which == 0 else ("core",))
                arrived(s, above, yy, c)
                forward(s, above, yy, ("down", "core") if d < 3 or which == 1 else ("core",))
        else:
            for yy in (yh, 1 - yh):
                arrived(s, plane(4), yy, c)
                forward(s, plane(4), yy, ("core",))

    def p_copy(s, zz):
        return remote(
            ps.at[s, zz], pr.at[s, mp], p_ss.at[s, zz], p_rs.at[s, mp], {"dp": me, "mp": zz}
        )

    def project(s, d):
        planes = (z,) if d == 0 else (plane(4),) if d == 4 else (plane(-d), plane(d))
        for zz in planes:
            for yy in range(2):
                arrived(s, zz, yy, 1 - c)
        rows = [g[s, zz].reshape(4 * RB, COLS) for zz in planes]
        rows = rows[0] if len(rows) == 1 else jnp.concatenate(rows, axis=0)
        product = jnp.dot(rows, w[...], preferred_element_type=F32).astype(BF16)
        for i, zz in enumerate(planes):
            part = product[i * 4 * RB : (i + 1) * 4 * RB]

            @pl.when(zz != mp)
            def _():
                ps[s, zz] = part
                p_copy(s, zz).start()

            @pl.when(zz == mp)
            def _():
                pr[s, mp] = part

    def finish(s):
        for j in range(MP):

            @pl.when(mp != j)
            def _():
                remote(
                    ps.at[s, 0], pr.at[s, j], p_ss.at[s, 0], p_rs.at[s, j], {"dp": me, "mp": j}
                ).wait_recv()

        total = pr[s, 0].astype(F32)
        for j in range(1, MP):
            total = total + pr[s, j].astype(F32)
        total = total.astype(BF16)
        for i in range(4):
            out[pl.ds(i * ROWS * STEPS + s * RB, RB), :] = total[i * RB : (i + 1) * RB]

    for s in range(ROUNDS):
        merge(s)
    loads[4].wait()
    order = sorted((2 * s + d, s, d) for s in range(ROUNDS) for d in range(5))
    for i, (_, s, d) in enumerate(order):
        ring(s, d)
        if i > 0:
            project(*order[i - 1][1:])
    project(*order[-1][1:])
    for s in range(ROUNDS):
        finish(s)

    for s in range(ROUNDS):
        q_copy(s).wait_send()
        t_copy(s).wait_send()
        st_copy(s).wait_send()
    for copy in sent:
        copy.wait_send()
    for s in range(ROUNDS):
        for j in range(MP):

            @pl.when(mp != j)
            def _():
                p_copy(s, j).wait_send()


def attention(bit, lengths, *arrays):
    any_space = pl.BlockSpec(memory_space=pl.ANY)
    vmem = pl.BlockSpec(memory_space=pltpu.VMEM)
    dma = pltpu.SemaphoreType.DMA
    return pl.pallas_call(
        functools.partial(kernel, bit),
        name=f"attention_{bit}",
        out_shape=jax.ShapeDtypeStruct((4 * ROWS * STEPS, OUT_COLS), BF16),
        in_specs=[pl.BlockSpec(memory_space=pltpu.SMEM)] + [vmem] * 3 + [any_space] * 5,
        out_specs=vmem,
        scratch_shapes=[
            *[pltpu.VMEM((ROWS, CAP, HEAD), BF16)] * 4,
            pltpu.VMEM((COLS, OUT_COLS), BF16),
            pltpu.VMEM((ROUNDS, QB, HEAD), BF16),
            pltpu.VMEM((ROUNDS, QB, HEAD), BF16),
            pltpu.VMEM((ROUNDS, RPR, QR, HEAD), F32),
            pltpu.VMEM((ROUNDS, RPR, QR, 1), F32),
            pltpu.VMEM((ROUNDS, RPR, QR, 1), F32),
            pltpu.VMEM((ROUNDS, QB, HEAD), BF16),
            pltpu.VMEM((ROUNDS, 8, HEAD), F32),
            pltpu.VMEM((ROUNDS, QB, HEAD), BF16),
            pltpu.VMEM((ROUNDS, 8, HEAD), F32),
            pltpu.VMEM((ROUNDS, Z, 2, 2, RB, COLS), BF16),
            pltpu.VMEM((ROUNDS, MP, 4 * RB, OUT_COLS), BF16),
            pltpu.VMEM((ROUNDS, MP, 4 * RB, OUT_COLS), BF16),
            dma((5,)),
            *[dma((ROUNDS,))] * 6,
            dma((ROUNDS, 2, Z, 2)),
            dma((ROUNDS, Z, 2)),
            dma((ROUNDS, Z, 2)),
            dma((ROUNDS, Z, 2, 2)),
            dma((ROUNDS, MP)),
            dma((ROUNDS, MP)),
        ],
        compiler_params=pltpu.CompilerParams(
            collective_id=bit + 1, has_side_effects=True, vmem_limit_bytes=48 << 20
        ),
    )(lengths, *arrays)


def body(
    queries, new_keys, new_values, key_cache, value_cache, key_spill, value_spill,
    lengths, partner, out_weight,
):
    rows = ROWS * STEPS
    arrays = (
        lengths,
        queries.reshape(rows, COLS),
        new_keys.reshape(rows, HEAD),
        new_values.reshape(rows, HEAD),
        *[a.reshape(ROWS, CAP, HEAD) for a in (key_cache, value_cache, key_spill, value_spill)],
        out_weight,
    )
    mask = partner[0]
    levels = lax.axis_size("dp").bit_length() - 1
    bit = sum((mask >= 2**level).astype(jnp.int32) for level in range(1, levels))
    return lax.switch(bit, [functools.partial(attention, b) for b in range(levels)], *arrays)


def solution(mesh):
    return jax.shard_map(
        body,
        mesh=mesh,
        in_specs=(
            P("dp", None, "mp"),
            P("dp", None, "mp"),
            P("dp", None, "mp"),
            P("dp", "mp", None, None),
            P("dp", "mp", None, None),
            P("dp", "mp", None, None),
            P("dp", "mp", None, None),
            P(),
            P(),
            P("mp", "dp"),
        ),
        out_specs=P("mp", "dp"),
        check_vma=False,
    )
```

```python
import functools
import math

import jax
import jax.numpy as jnp
from jax import lax
from jax.experimental import pallas as pl
from jax.experimental.pallas import tpu as pltpu
from jax.sharding import PartitionSpec as P

MESH = pl.DeviceIdType.MESH
MASKED = -1e30
F32, BF16 = jnp.float32, jnp.bfloat16

ROWS = 16
STEPS = 4
GROUP = 12
HEAD = 128
CAP = 128
COLS = GROUP * HEAD
OUT_COLS = 384
ROUNDS = 4
RPR = ROWS // ROUNDS
RB = RPR * STEPS
QR = GROUP * STEPS
QB = RPR * QR
Z, X = 8, 4
PIECES = ((0, 256), (256, 128))
SCALE2 = math.log2(math.e) / math.sqrt(HEAD)


def kernel(
    bit,
    lengths_hbm, q_hbm, nk_hbm, nv_hbm, k_hbm, v_hbm, sk_hbm, sv_hbm, w_hbm,
    out,
    lengths, q_own, nk, nv, k, v, sk, sv, w, w_far, q_far, o_own, m_own, l_own,
    t_send, st_send, t_recv, st_recv, g, ps, px, py_send, py, pf, po,
    load_sem, q_ss, q_rs, t_ss, t_rs, st_ss, st_rs, w_ss, w_rs, z_ss, c_ss, g_rs,
    px_ss, px_rs, py_ss, py_rs, po_ss, po_rs,
):
    me, mp = lax.axis_index("dp"), lax.axis_index("mp")
    z, yh, c = me // 4, (me // 2) % 2, me % 2
    x, yl = mp // 2, mp % 2
    mask = 2**bit
    partner = me + mask * (1 - 2 * ((me // mask) % 2))

    def plane(d):
        return lax.rem(z + d + Z, Z)

    def along_z(d):
        return {"dp": plane(d) * 4 + yh * 2 + c, "mp": mp}

    def along_y(hi, lo):
        return {"dp": z * 4 + hi * 2 + c, "mp": x * 2 + lo}

    far = {"dp": partner, "mp": mp}
    sibling = {"dp": z * 4 + yh * 2 + 1 - c, "mp": mp}

    loads = [
        pltpu.make_async_copy(src, dst, load_sem.at[i])
        for i, (src, dst) in enumerate(
            [
                (q_hbm, q_own), (lengths_hbm, lengths), (nk_hbm, nk), (nv_hbm, nv), (k_hbm, k), (v_hbm, v),
                (sk_hbm, sk), (sv_hbm, sv), (w_hbm, w),
            ]
        )
    ]
    for load in loads:
        load.start()

    barrier = pltpu.get_barrier_semaphore()
    peers = [{"dp": me, "mp": lax.rem(x + j, X) * 2 + yl} for j in range(1, X)]
    peers += [{"dp": z * 4 + (1 - yh) * 2 + c, "mp": j} for j in range(2 * X)]
    greeted = [along_z(d) for d in (1, -1, 2, -2)] + [sibling, far, along_y(yh, 1 - yl)] + peers
    for device in greeted:
        pl.semaphore_signal(barrier, inc=1, device_id=device, device_id_type=MESH)
    pl.semaphore_wait(barrier, len(greeted))

    def remote(src, dst, send_sem, recv_sem, device):
        return pltpu.make_async_remote_copy(
            src_ref=src, dst_ref=dst, send_sem=send_sem, recv_sem=recv_sem,
            device_id=device, device_id_type=MESH,
        )

    def q_copy(s):
        return remote(q_hbm.at[s], q_far.at[s], q_ss.at[s], q_rs.at[s], far)

    def t_copy(s):
        return remote(t_send.at[s], t_recv.at[s], t_ss.at[s], t_rs.at[s], far)

    def st_copy(s):
        return remote(st_send.at[s], st_recv.at[s], st_ss.at[s], st_rs.at[s], far)

    def w_copy(i):
        columns = pl.ds(*PIECES[i // 4])
        rows = pl.ds(0, COLS) if i == 4 else pl.ds(i * (COLS // 4), COLS // 4)
        return remote(
            w_hbm.at[rows, columns], w_far.at[rows, columns], w_ss.at[i], w_rs.at[i], along_y(1 - yh, yl)
        )

    for s in range(ROUNDS):
        q_copy(s).start()
    if bit != 1:
        for i in range(4):
            w_copy(i).start()
    for load in loads:
        load.wait()

    lane = lax.broadcasted_iota(jnp.int32, (1, CAP), 1)

    def bias_of(owner, s, less):
        return jnp.stack(
            [
                jnp.where(lane < lengths[owner * ROWS + s * RPR + r] - less, 0.0, MASKED)
                for r in range(RPR)
            ]
        )

    def scores_of(queries, keys, bias):
        raw = jnp.einsum("rqd,rkd->rqk", queries, keys, preferred_element_type=F32)
        return raw * SCALE2 + bias

    def own(s):
        q_row = lax.broadcasted_iota(jnp.int32, (QB, RB), 0)
        f_col = lax.broadcasted_iota(jnp.int32, (QB, RB), 1)
        first = (f_col >> 2) * QR
        fresh_ok = (q_row >= first) & (q_row < first + QR) & ((f_col & 3) <= (q_row & 3))
        fresh_bias = jnp.where(fresh_ok, 0.0, MASKED)
        rows = pl.ds(s * RPR, RPR)
        queries = q_own[s]
        cached = scores_of(queries.reshape(RPR, QR, HEAD), k[rows], bias_of(me, s, 0))
        fresh = lax.dot_general(
            queries, nk[s], (((1,), (1,)), ((), ())), preferred_element_type=F32
        )
        fresh = (fresh * SCALE2 + fresh_bias).reshape(RPR, QR, RB)
        peak = jnp.maximum(
            jnp.max(cached, axis=-1, keepdims=True), jnp.max(fresh, axis=-1, keepdims=True)
        )
        cached, fresh = jnp.exp2(cached - peak), jnp.exp2(fresh - peak)
        m_own[s] = peak
        l_own[s] = jnp.sum(cached, axis=-1, keepdims=True) + jnp.sum(fresh, axis=-1, keepdims=True)
        summed = jnp.einsum("rqk,rkd->rqd", cached.astype(BF16), v[rows], preferred_element_type=F32)
        o_own[s] = summed + jnp.dot(
            fresh.astype(BF16).reshape(QB, RB), nv[s], preferred_element_type=F32
        ).reshape(RPR, QR, HEAD)

    def diagonal():
        shape = (RPR, QR, CAP)
        return lax.broadcasted_iota(jnp.int32, shape, 1) == lax.broadcasted_iota(jnp.int32, shape, 2)

    def tail(s):
        rows = pl.ds(s * RPR, RPR)
        q_copy(s).wait_recv()
        scores = scores_of(q_far[s].reshape(RPR, QR, HEAD), sk[rows], bias_of(partner, s, CAP))
        peak = jnp.max(scores, axis=-1, keepdims=True)
        scores = jnp.exp2(scores - peak)
        weight = jnp.sum(scores, axis=-1, keepdims=True)
        summed = jnp.einsum("rqk,rkd->rqd", scores.astype(BF16), sv[rows], preferred_element_type=F32)
        t_send[s] = (summed / weight).astype(BF16).reshape(QB, HEAD)
        t_copy(s).start()
        st_send[s, 0:RPR] = jnp.sum(jnp.where(diagonal(), peak + jnp.log2(weight), 0.0), axis=1)
        st_copy(s).start()

        for i in range(ROUNDS):

            @pl.when(s == i)
            def _():
                if bit == 1:
                    w_copy(i).start()
                if i == ROUNDS - 1:
                    w_copy(4).start()

    def along(s, zz, d):
        ref = g.at[s, zz, c]
        return remote(ref, ref, z_ss.at[s, zz, d + 2], g_rs.at[s, zz, c], along_z(d))

    def to_core(s, zz):
        ref = g.at[s, zz, c]
        return remote(ref, ref, c_ss.at[s, zz], g_rs.at[s, zz, c], sibling)

    def arrived(s, zz, cc):
        ref = g.at[s, zz, cc]
        remote(ref, ref, c_ss.at[s, zz], g_rs.at[s, zz, cc], sibling).wait_recv()

    def merge(s):
        t_copy(s).wait_recv()
        st_copy(s).wait_recv()
        log_sum = jnp.sum(
            jnp.where(diagonal(), st_recv[s, 0:RPR][:, None, :], 0.0), axis=-1, keepdims=True
        )
        peak = jnp.maximum(m_own[s], log_sum)
        near_factor, far_factor = jnp.exp2(m_own[s] - peak), jnp.exp2(log_sum - peak)
        far_part = t_recv[s].reshape(RPR, QR, HEAD).astype(F32)
        total = near_factor * o_own[s] + far_factor * far_part
        context = (total / (near_factor * l_own[s] + far_factor)).astype(BF16)
        index = lax.broadcasted_iota(jnp.int32, (QB, QB), 0)
        source = ((index >> 2) & 3) * QR + (index >> 4) * STEPS + (index & 3)
        one_hot = jnp.where(lax.broadcasted_iota(jnp.int32, (QB, QB), 1) == source, 1.0, 0.0)
        heads = jnp.dot(
            one_hot.astype(BF16), context.reshape(QB, HEAD), preferred_element_type=F32
        ).astype(BF16)
        for h in range(GROUP):
            g[s, z, c, :, h * HEAD : (h + 1) * HEAD] = heads[h * RB : (h + 1) * RB]
        for d in (1, -1):
            along(s, z, d).start()
        to_core(s, z).start()

    def ring(s, d):
        for zz, away in ((plane(-d), 1), (plane(d), -1)):
            arrived(s, zz, c)
            if d < 3:
                along(s, zz, away).start()
            if d == 2:

                @pl.when(lax.rem(s, 2) == (1 - away) // 2)
                def _():
                    along(s, zz, 2 * away).start()

            to_core(s, zz).start()
        if d == 3:
            arrived(s, plane(4), c)
            to_core(s, plane(4)).start()

    def px_copy(s, zz):
        device = {"dp": me, "mp": (zz // 2) * 2 + yl}
        return remote(
            ps.at[s, zz], px.at[s, zz % 2, x], px_ss.at[s, zz], px_rs.at[s, zz % 2, x], device
        )

    def py_copy(s):
        return remote(py_send.at[s], py.at[s], py_ss.at[s], py_rs.at[s], along_y(yh, 1 - yl))

    def po_copy(s, zz, i):
        device = {"dp": z * 4 + (1 - yh) * 2 + c, "mp": zz}
        columns = pl.ds(*PIECES[i])
        return remote(
            pf.at[s, zz, :, columns], po.at[s, mp, :, columns], po_ss.at[s, zz, i], po_rs.at[s, mp, i], device
        )

    def product(s, distances, weight):
        planes = [plane(d) for d in distances]
        rows = jnp.concatenate([g[s, zz].reshape(2 * RB, COLS) for zz in planes], axis=0)
        whole = jnp.dot(rows, weight, preferred_element_type=F32).astype(BF16)
        return [(zz, whole[i * 2 * RB : (i + 1) * 2 * RB]) for i, zz in enumerate(planes)]

    def project(s, distances):
        for d in distances:
            arrived(s, plane(d), 1 - c)
        for zz, part in product(s, distances, w[...]):

            @pl.when(zz // 2 != x)
            def _():
                ps[s, zz] = part
                px_copy(s, zz).start()

            @pl.when(zz // 2 == x)
            def _():
                px[s, zz % 2, x] = part

    def project_far(s, distances, i):
        start, size = PIECES[i]
        for zz, part in product(s, distances, w_far[:, start : start + size]):
            pf[s, zz, :, start : start + size] = part
            po_copy(s, zz, i).start()

    def sum_x(s, lo):
        for j in range(X):

            @pl.when(x != j)
            def _():
                ref, sem = px.at[s, lo, j], px_rs.at[s, lo, j]
                remote(ref, ref, px_ss.at[s, 0], sem, sibling).wait_recv()

        total = px[s, lo, 0].astype(F32)
        for j in range(1, X):
            total = total + px[s, lo, j].astype(F32)
        return total

    def store(s, hi, total):
        for i in range(2):
            start = (hi * 2 + i) * ROWS * STEPS + s * RB
            out[pl.ds(pl.multiple_of(start, RB), RB), :] = total[i * RB : (i + 1) * RB].astype(BF16)

    def hand_over(s):
        py_send[s] = sum_x(s, 1 - yl).astype(BF16)
        py_copy(s).start()

    def finish(s):
        total = sum_x(s, yl)
        py_copy(s).wait_recv()
        store(s, yh, total + py[s].astype(F32))

    def finish_far(s, carry):
        for i in range(2):
            for j in range(2 * X):
                ref, sem = po.at[s, j, :, pl.ds(*PIECES[i])], po_rs.at[s, j, i]
                remote(ref, ref, po_ss.at[s, 0, i], sem, sibling).wait_recv()
        total = po[s, 0].astype(F32)
        for j in range(1, 2 * X):
            total = total + po[s, j].astype(F32)
        store(s, 1 - yh, total)
        return carry

    inner, outer = (0, -1, 1, -2, 2), (-3, 3, 4)
    last = ROUNDS - 1
    stages = [
        (0, own), (0, tail), (1, merge),
        *[(1 + d, functools.partial(ring, d=d)) for d in (1, 2, 3)],
        (4, functools.partial(project, distances=outer)),
        (3, functools.partial(project, distances=inner)),
        (5, hand_over), (6, finish),
    ]

    def slot(t, carry):
        for behind, stage in stages:
            s = t - behind

            @pl.when((s >= 0) & (s < ROUNDS))
            def _():
                stage(s)

        @pl.when(t == 4)
        def _():
            for i in range(4):
                w_copy(i).wait_recv()

        @pl.when((t >= 4) & (t < 4 + last))
        def _():
            project_far(t - 4, inner + outer, 0)

        @pl.when(t == 3 + last)
        def _():
            project_far(last, inner, 0)
            w_copy(4).wait_recv()

        @pl.when(t == 4 + last)
        def _():
            project_far(last, outer, 0)

        @pl.when((t == 3 + last) | (t == 4 + last))
        def _():
            def second(s, carry):
                project_far(s, inner + outer, 1)
                return carry

            late = t - 3 - last
            lax.fori_loop(late * last, last + late, second, 0)

        return carry

    lax.fori_loop(0, ROUNDS + max(behind for behind, _ in stages), slot, 0)
    lax.fori_loop(0, ROUNDS, finish_far, 0)

    def drain(s, carry):
        q_copy(s).wait_send()
        t_copy(s).wait_send()
        st_copy(s).wait_send()
        for away in (1, -1):
            for d in range(3):
                along(s, plane(-d * away), away).wait_send()

            @pl.when(lax.rem(s, 2) == (1 - away) // 2)
            def _():
                along(s, plane(-2 * away), 2 * away).wait_send()

        py_copy(s).wait_send()
        for zz in range(Z):
            to_core(s, zz).wait_send()
            for i in range(2):
                po_copy(s, zz, i).wait_send()

            @pl.when(zz // 2 != x)
            def _():
                px_copy(s, zz).wait_send()

        return carry

    lax.fori_loop(0, ROUNDS, drain, 0)
    for i in range(5):
        w_copy(i).wait_send()


def attention(bit, *arrays):
    any_space = pl.BlockSpec(memory_space=pl.ANY)
    dma = pltpu.SemaphoreType.DMA
    return pl.pallas_call(
        functools.partial(kernel, bit),
        name=f"attention_{bit}",
        out_shape=jax.ShapeDtypeStruct((4 * ROWS * STEPS, OUT_COLS), BF16),
        in_specs=[any_space] * 9,
        out_specs=pl.BlockSpec(memory_space=pltpu.VMEM),
        scratch_shapes=[
            pltpu.SMEM((ROWS * 32,), jnp.int32),
            pltpu.VMEM((ROUNDS, QB, HEAD), BF16),
            *[pltpu.VMEM((ROUNDS, RB, HEAD), BF16)] * 2,
            *[pltpu.VMEM((ROWS, CAP, HEAD), BF16)] * 4,
            *[pltpu.VMEM((COLS, OUT_COLS), BF16)] * 2,
            pltpu.VMEM((ROUNDS, QB, HEAD), BF16),
            pltpu.VMEM((ROUNDS, RPR, QR, HEAD), F32),
            pltpu.VMEM((ROUNDS, RPR, QR, 1), F32),
            pltpu.VMEM((ROUNDS, RPR, QR, 1), F32),
            pltpu.VMEM((ROUNDS, QB, HEAD), BF16),
            pltpu.VMEM((ROUNDS, 8, HEAD), F32),
            pltpu.VMEM((ROUNDS, QB, HEAD), BF16),
            pltpu.VMEM((ROUNDS, 8, HEAD), F32),
            pltpu.VMEM((ROUNDS, Z, 2, RB, COLS), BF16),
            pltpu.VMEM((ROUNDS, Z, 2 * RB, OUT_COLS), BF16),
            pltpu.VMEM((ROUNDS, 2, X, 2 * RB, OUT_COLS), BF16),
            pltpu.VMEM((ROUNDS, 2 * RB, OUT_COLS), BF16),
            pltpu.VMEM((ROUNDS, 2 * RB, OUT_COLS), BF16),
            pltpu.VMEM((ROUNDS, Z, 2 * RB, OUT_COLS), BF16),
            pltpu.VMEM((ROUNDS, 2 * X, 2 * RB, OUT_COLS), BF16),
            dma((9,)),
            *[dma((ROUNDS,))] * 6,
            *[dma((5,))] * 2,
            dma((ROUNDS, Z, 5)),
            dma((ROUNDS, Z)),
            dma((ROUNDS, Z, 2)),
            dma((ROUNDS, Z)),
            dma((ROUNDS, 2, X)),
            *[dma((ROUNDS,))] * 2,
            *[dma((ROUNDS, Z, 2))] * 2,
        ],
        compiler_params=pltpu.CompilerParams(
            collective_id=bit + 1, has_side_effects=True, vmem_limit_bytes=48 << 20
        ),
    )(*arrays)


def body(
    queries, new_keys, new_values, key_cache, value_cache, key_spill, value_spill,
    lengths, partner, out_weight,
):
    by_head = queries.reshape(ROWS, STEPS, GROUP, HEAD).transpose(0, 2, 1, 3)
    arrays = (
        lengths,
        by_head.reshape(ROUNDS, QB, HEAD),
        new_keys.reshape(ROUNDS, RB, HEAD),
        new_values.reshape(ROUNDS, RB, HEAD),
        *[a.reshape(ROWS, CAP, HEAD) for a in (key_cache, value_cache, key_spill, value_spill)],
        out_weight,
    )
    levels = lax.axis_size("dp").bit_length() - 1
    bit = 31 - lax.clz(partner[0])
    return lax.switch(bit, [functools.partial(attention, b) for b in range(levels)], *arrays)


def solution(mesh):
    return jax.shard_map(
        body,
        mesh=mesh,
        in_specs=(
            P("dp", None, "mp"),
            P("dp", None, "mp"),
            P("dp", None, "mp"),
            P("dp", "mp", None, None),
            P("dp", "mp", None, None),
            P("dp", "mp", None, None),
            P("dp", "mp", None, None),
            P(),
            P(),
            P("mp", "dp"),
        ),
        out_specs=P("mp", "dp"),
        check_vma=False,
    )
```

```python
import functools
import math

import jax
import jax.numpy as jnp
from jax import lax
from jax.experimental import pallas as pl
from jax.experimental.pallas import tpu as pltpu
from jax.sharding import PartitionSpec as P

MESH = pl.DeviceIdType.MESH
MASKED = -1e30
F32, BF16 = jnp.float32, jnp.bfloat16

ROWS = 16
STEPS = 4
GROUP = 12
HEAD = 128
CAP = 128
COLS = GROUP * HEAD
OUT_COLS = 384
ROUNDS = 4
RPR = ROWS // ROUNDS
RB = RPR * STEPS
QR = GROUP * STEPS
QB = RPR * QR
Z, X = 8, 4
PIECES = ((0, OUT_COLS), (OUT_COLS, 256), (OUT_COLS + 256, 128))
LAST = ROUNDS - 1
LAG = (1, 1, 1, 2, 2)
HANDED = ((0, OUT_COLS), (0, 256), (256, 128))
SCALE2 = math.log2(math.e) / math.sqrt(HEAD)


def kernel(
    bit,
    lengths_hbm, q_hbm, nk_hbm, nv_hbm, k_hbm, v_hbm, sk_hbm, sv_hbm, w_hbm,
    out,
    lengths, q_own, nk, nv, k, v, sk, sv, w, w_far, q_far, o_own, m_own, l_own,
    t_send, st_send, t_recv, st_recv, g, ps, px, py_send, py,
    load_sem, q_ss, q_rs, t_ss, t_rs, st_ss, st_rs, w_ss, w_rs, z_ss, z_rs, c_ss, c_rs,
    px_ss, px_rs, py_ss, py_rs,
):
    me, mp = lax.axis_index("dp"), lax.axis_index("mp")
    z, yh, c = me // 4, (me // 2) % 2, me % 2
    x, yl = mp // 2, mp % 2
    mask = 2**bit
    partner = me + mask * (1 - 2 * ((me // mask) % 2))

    def plane(d):
        return lax.rem(z + d + Z, Z)

    def along_z(d):
        return {"dp": plane(d) * 4 + yh * 2 + c, "mp": mp}

    def along_y(hi, lo):
        return {"dp": z * 4 + hi * 2 + c, "mp": x * 2 + lo}

    far = {"dp": partner, "mp": mp}
    sibling = {"dp": z * 4 + yh * 2 + 1 - c, "mp": mp}

    loads = [
        pltpu.make_async_copy(src, dst, load_sem.at[i])
        for i, (src, dst) in enumerate(
            [
                (q_hbm, q_own), (lengths_hbm, lengths), (nk_hbm, nk), (nv_hbm, nv), (k_hbm, k), (v_hbm, v),
                (sk_hbm, sk), (sv_hbm, sv), (w_hbm, w),
            ]
        )
    ]
    for load in loads:
        load.start()

    barrier = pltpu.get_barrier_semaphore()
    peers = [{"dp": me, "mp": lax.rem(x + j, X) * 2 + yl} for j in range(1, X)]
    column = [along_y(yh, 1 - yl), along_y(1 - yh, 0), along_y(1 - yh, 1)]
    greeted = [along_z(d) for d in (1, -1, 2, -2)] + [sibling, far] + column + peers
    for device in greeted:
        pl.semaphore_signal(barrier, inc=1, device_id=device, device_id_type=MESH)
    pl.semaphore_wait(barrier, len(greeted))

    def remote(src, dst, send_sem, recv_sem, device):
        return pltpu.make_async_remote_copy(
            src_ref=src, dst_ref=dst, send_sem=send_sem, recv_sem=recv_sem,
            device_id=device, device_id_type=MESH,
        )

    def q_copy(s):
        return remote(q_hbm.at[s], q_far.at[s], q_ss.at[s], q_rs.at[s], far)

    def t_copy(s):
        return remote(t_send.at[s], t_recv.at[s], t_ss.at[s], t_rs.at[s], far)

    def st_copy(s):
        return remote(st_send.at[s], st_recv.at[s], st_ss.at[s], st_rs.at[s], far)

    def w_copy(i):
        columns = pl.ds(256, 128) if i == 4 else pl.ds(0, 256)
        rows = pl.ds(0, COLS) if i == 4 else pl.ds(i * (COLS // 4), COLS // 4)
        return remote(
            w_hbm.at[rows, columns], w_far.at[rows, columns], w_ss.at[i], w_rs.at[i], along_y(1 - yh, yl)
        )

    for s in range(ROUNDS):
        q_copy(s).start()
    if bit != 1:
        for i in range(4):
            w_copy(i).start()
    for load in loads:
        load.wait()

    lane = lax.broadcasted_iota(jnp.int32, (1, CAP), 1)

    def bias_of(owner, s, less):
        return jnp.stack(
            [
                jnp.where(lane < lengths[owner * ROWS + s * RPR + r] - less, 0.0, MASKED)
                for r in range(RPR)
            ]
        )

    def scores_of(queries, keys, bias):
        raw = jnp.einsum("rqd,rkd->rqk", queries, keys, preferred_element_type=F32)
        return raw * SCALE2 + bias

    def own(s):
        q_row = lax.broadcasted_iota(jnp.int32, (QB, RB), 0)
        f_col = lax.broadcasted_iota(jnp.int32, (QB, RB), 1)
        first = (f_col >> 2) * QR
        fresh_ok = (q_row >= first) & (q_row < first + QR) & ((f_col & 3) <= (q_row & 3))
        fresh_bias = jnp.where(fresh_ok, 0.0, MASKED)
        rows = pl.ds(s * RPR, RPR)
        queries = q_own[s]
        cached = scores_of(queries.reshape(RPR, QR, HEAD), k[rows], bias_of(me, s, 0))
        fresh = lax.dot_general(
            queries, nk[s], (((1,), (1,)), ((), ())), preferred_element_type=F32
        )
        fresh = (fresh * SCALE2 + fresh_bias).reshape(RPR, QR, RB)
        peak = jnp.maximum(
            jnp.max(cached, axis=-1, keepdims=True), jnp.max(fresh, axis=-1, keepdims=True)
        )
        cached, fresh = jnp.exp2(cached - peak), jnp.exp2(fresh - peak)
        m_own[s] = peak
        l_own[s] = jnp.sum(cached, axis=-1, keepdims=True) + jnp.sum(fresh, axis=-1, keepdims=True)
        summed = jnp.einsum("rqk,rkd->rqd", cached.astype(BF16), v[rows], preferred_element_type=F32)
        o_own[s] = summed + jnp.dot(
            fresh.astype(BF16).reshape(QB, RB), nv[s], preferred_element_type=F32
        ).reshape(RPR, QR, HEAD)

    def diagonal():
        shape = (RPR, QR, CAP)
        return lax.broadcasted_iota(jnp.int32, shape, 1) == lax.broadcasted_iota(jnp.int32, shape, 2)

    def tail(s):
        rows = pl.ds(s * RPR, RPR)
        q_copy(s).wait_recv()
        scores = scores_of(q_far[s].reshape(RPR, QR, HEAD), sk[rows], bias_of(partner, s, CAP))
        peak = jnp.max(scores, axis=-1, keepdims=True)
        scores = jnp.exp2(scores - peak)
        weight = jnp.sum(scores, axis=-1, keepdims=True)
        summed = jnp.einsum("rqk,rkd->rqd", scores.astype(BF16), sv[rows], preferred_element_type=F32)
        t_send[s] = (summed / weight).astype(BF16).reshape(QB, HEAD)
        t_copy(s).start()
        st_send[s, 0:RPR] = jnp.sum(jnp.where(diagonal(), peak + jnp.log2(weight), 0.0), axis=1)
        st_copy(s).start()

        for i in range(ROUNDS):

            @pl.when(s == i)
            def _():
                if bit == 1:
                    w_copy(i).start()
                if i == ROUNDS - 1:
                    w_copy(4).start()

    def along(s, zz, d):
        ref = g.at[s, zz, c]
        return remote(ref, ref, z_ss.at[s], z_rs.at[s, zz], along_z(d))

    def to_core(s, zz, half):
        ref = g.at[s, zz, c]
        return remote(ref, ref, c_ss.at[s], c_rs.at[s, half], sibling)

    def merge(s):
        t_copy(s).wait_recv()
        st_copy(s).wait_recv()
        log_sum = jnp.sum(
            jnp.where(diagonal(), st_recv[s, 0:RPR][:, None, :], 0.0), axis=-1, keepdims=True
        )
        peak = jnp.maximum(m_own[s], log_sum)
        near_factor, far_factor = jnp.exp2(m_own[s] - peak), jnp.exp2(log_sum - peak)
        far_part = t_recv[s].reshape(RPR, QR, HEAD).astype(F32)
        total = near_factor * o_own[s] + far_factor * far_part
        context = (total / (near_factor * l_own[s] + far_factor)).astype(BF16)
        index = lax.broadcasted_iota(jnp.int32, (QB, QB), 0)
        source = ((index >> 2) & 3) * QR + (index >> 4) * STEPS + (index & 3)
        one_hot = jnp.where(lax.broadcasted_iota(jnp.int32, (QB, QB), 1) == source, 1.0, 0.0)
        heads = jnp.dot(
            one_hot.astype(BF16), context.reshape(QB, HEAD), preferred_element_type=F32
        ).astype(BF16)
        for h in range(GROUP):
            g[s, z, c, :, h * HEAD : (h + 1) * HEAD] = heads[h * RB : (h + 1) * RB]
        for d in (1, -1):
            along(s, z, d).start()

        to_core(s, z, 0).start()

    def ring(s, d):
        for zz, away in ((plane(-d), 1), (plane(d), -1)):
            along(s, zz, 1).wait_recv()
            if d < 3:
                along(s, zz, away).start()
            if d == 2:

                @pl.when(lax.rem(s, 2) == (1 - away) // 2)
                def _():
                    along(s, zz, 2 * away).start()

            to_core(s, zz, d // 3).start()
        if d == 3:
            along(s, plane(4), 1).wait_recv()
            to_core(s, plane(4), 1).start()

    def px_copy(s, j, i):
        columns = pl.ds(*PIECES[i])
        return remote(
            ps.at[s, pl.ds(2 * j, 2), :, columns], px.at[s, x, :, :, columns],
            px_ss.at[s, i], px_rs.at[s, i], {"dp": me, "mp": 2 * j + yl},
        )

    def px_arrived(s, i):
        ref = px.at[s, pl.ds(0, X - 1), :, :, pl.ds(*PIECES[i])]
        remote(ref, ref, px_ss.at[s, i], px_rs.at[s, i], sibling).wait_recv()

    def py_copy(s, k, i):
        device = along_y(1 - yh, k - 1) if k else along_y(yh, 1 - yl)
        columns = pl.ds(*HANDED[i])
        return remote(
            py_send.at[s, k, :, columns], py.at[s, 1 + yl if k else 0, :, columns],
            py_ss.at[s, i], py_rs.at[s, i], device,
        )

    def py_parts(ref, s, i):
        return ref.at[s, pl.ds(1, 2) if i else 0, :, pl.ds(*HANDED[i])]

    def project(s, weights, i):
        rows = g[s].reshape(Z * 2 * RB, COLS)
        start = PIECES[i][0]
        for weight in weights:
            product = jnp.dot(rows, weight, preferred_element_type=F32).astype(BF16)
            columns = slice(start, start + weight.shape[1])
            start += weight.shape[1]
            product = product.reshape(Z, 2 * RB, weight.shape[1])
            ps[s, :, :, columns] = product
            for j in range(X):

                @pl.when(x == j)
                def _():
                    px[s, j, :, :, columns] = product[2 * j : 2 * j + 2]

        for j in range(X):

            @pl.when(x != j)
            def _():
                px_copy(s, j, i).start()

    inner, outer = (0, -1, 1, -2, 2), (-3, 3, 4)

    def plane_copy(s, zz):
        columns = pl.ds(*PIECES[0])
        return remote(
            ps.at[s, zz, :, columns], px.at[s, x, lax.rem(zz, 2), :, columns],
            px_ss.at[s, 0], px_rs.at[s, 0], {"dp": me, "mp": (zz // 2) * 2 + yl},
        )

    def project_own(s, distances):
        half = int(distances == outer)
        ref = g.at[s, pl.ds(0, len(distances)), 1 - c]
        remote(ref, ref, c_ss.at[s], c_rs.at[s, half], sibling).wait_recv()
        planes = [plane(d) for d in distances]
        rows = jnp.concatenate([g[s, zz].reshape(2 * RB, COLS) for zz in planes], axis=0)
        product = jnp.dot(rows, w[...], preferred_element_type=F32).astype(BF16)
        for j, zz in enumerate(planes):
            mine = product[j * 2 * RB : (j + 1) * 2 * RB]

            @pl.when(zz // 2 != x)
            def _():
                ps[s, zz, :, :OUT_COLS] = mine
                plane_copy(s, zz).start()

            @pl.when(zz // 2 == x)
            def _():
                px[s, x, lax.rem(zz, 2), :, :OUT_COLS] = mine

    def project_first(s):
        @pl.when(s == 0)
        def _():
            for i in range(4):
                w_copy(i).wait_recv()

        project(s, (w_far[:, :256],), 1)

    def project_second(s):
        @pl.when(s == 0)
        def _():
            w_copy(4).wait_recv()

        project(s, (w_far[:, 256:],), 2)

    def sum_x(s, lo, columns):
        total = px[s, 0, lo, :, columns].astype(F32)
        for j in range(1, X):
            total = total + px[s, j, lo, :, columns].astype(F32)
        return total

    def hand_over(s, i):
        start, size = HANDED[i]
        offset = OUT_COLS if i else 0
        for k in (1, 2) if i else (0,):
            total = sum_x(s, k - 1 if k else 1 - yl, slice(offset + start, offset + start + size))
            py_send[s, k, :, start : start + size] = total.astype(BF16)
            py_copy(s, k, i).start()

    def hand_first(s):
        px_arrived(s, 0)
        hand_over(s, 0)
        px_arrived(s, 1)
        hand_over(s, 1)

    def hand_second(s):
        px_arrived(s, 2)
        hand_over(s, 2)

    def finish(s):
        for i in range(3):
            ref = py_parts(py, s, i)
            remote(ref, ref, py_ss.at[s, i], py_rs.at[s, i], sibling).wait_recv()
        own_rows = sum_x(s, yl, slice(0, OUT_COLS)) + py[s, 0].astype(F32)
        far_rows = py[s, 1].astype(F32) + py[s, 2].astype(F32)
        for hi, total in ((yh, own_rows), (1 - yh, far_rows)):
            for i in range(2):
                start = (hi * 2 + i) * ROWS * STEPS + s * RB
                part = total[i * RB : (i + 1) * RB].astype(BF16)
                out[pl.ds(pl.multiple_of(start, RB), RB), :] = part

    part, early = functools.partial, bit >= 3
    stages = [(own, (0, 1, 2, 3)), (tail, (0, 1, 2, 3))] + [
        (stage, tuple(at + LAG[bit] for at in slots))
        for stage, slots in (
            (merge, (0, 1, 2, 3)),
            (part(ring, d=1), (1, 2, 3, 4)),
            (part(ring, d=2), (2, 3, 4, 5)),
            (part(ring, d=3), (3, 4, 5, 6)),
            (part(project_own, distances=outer), (4, 5, 6, 6)),
            (part(project_own, distances=inner), (3, 4, 5, 5)),
            (project_first, (4, 5, 6, 6)),
            (hand_first, (7, 7, 7, 7) if early else (6, 6, 7, 7)),
            (project_second, (5, 5, 6, 6) if early else (6, 6, 6, 6)),
            (hand_second, (7, 7, 7, 7)),
            (finish, (8, 8, 8, 8)),
        )
    ]

    def slot(t, carry):
        for stage, slots in stages:

            def one(s, inside, stage=stage):
                stage(s)
                return inside

            begun = sum((t > at).astype(jnp.int32) for at in slots)
            due = sum((t >= at).astype(jnp.int32) for at in slots)
            lax.fori_loop(begun, due, one, 0)

        return carry

    lax.fori_loop(0, 1 + max(slots[-1] for _, slots in stages), slot, 0)

    def drain(s, carry):
        q_copy(s).wait_send()
        t_copy(s).wait_send()
        st_copy(s).wait_send()
        for ref, sem in (
            (g.at[s, pl.ds(0, 7), 0], z_ss.at[s]),
            (g.at[s, :, 0], c_ss.at[s]),
            *[(ps.at[s, pl.ds(0, 2 * X - 2), :, pl.ds(*PIECES[i])], px_ss.at[s, i]) for i in range(3)],
            *[(py_parts(py_send, s, i), py_ss.at[s, i]) for i in range(3)],
        ):
            remote(ref, ref, sem, c_rs.at[s, 0], sibling).wait_send()
        return carry

    lax.fori_loop(0, ROUNDS, drain, 0)
    for i in range(5):
        w_copy(i).wait_send()


def attention(bit, *arrays):
    any_space = pl.BlockSpec(memory_space=pl.ANY)
    dma = pltpu.SemaphoreType.DMA
    return pl.pallas_call(
        functools.partial(kernel, bit),
        name=f"attention_{bit}",
        out_shape=jax.ShapeDtypeStruct((4 * ROWS * STEPS, OUT_COLS), BF16),
        in_specs=[any_space] * 9,
        out_specs=pl.BlockSpec(memory_space=pltpu.VMEM),
        scratch_shapes=[
            pltpu.SMEM((ROWS * 32,), jnp.int32),
            pltpu.VMEM((ROUNDS, QB, HEAD), BF16),
            *[pltpu.VMEM((ROUNDS, RB, HEAD), BF16)] * 2,
            *[pltpu.VMEM((ROWS, CAP, HEAD), BF16)] * 4,
            *[pltpu.VMEM((COLS, OUT_COLS), BF16)] * 2,
            pltpu.VMEM((ROUNDS, QB, HEAD), BF16),
            pltpu.VMEM((ROUNDS, RPR, QR, HEAD), F32),
            pltpu.VMEM((ROUNDS, RPR, QR, 1), F32),
            pltpu.VMEM((ROUNDS, RPR, QR, 1), F32),
            pltpu.VMEM((ROUNDS, QB, HEAD), BF16),
            pltpu.VMEM((ROUNDS, 8, HEAD), F32),
            pltpu.VMEM((ROUNDS, QB, HEAD), BF16),
            pltpu.VMEM((ROUNDS, 8, HEAD), F32),
            pltpu.VMEM((ROUNDS, Z, 2, RB, COLS), BF16),
            pltpu.VMEM((ROUNDS, Z, 2 * RB, 2 * OUT_COLS), BF16),
            pltpu.VMEM((ROUNDS, X, 2, 2 * RB, 2 * OUT_COLS), BF16),
            pltpu.VMEM((ROUNDS, 3, 2 * RB, OUT_COLS), BF16),
            pltpu.VMEM((ROUNDS, 3, 2 * RB, OUT_COLS), BF16),
            dma((9,)),
            *[dma((ROUNDS,))] * 6,
            *[dma((5,))] * 2,
            dma((ROUNDS,)),
            dma((ROUNDS, Z)),
            dma((ROUNDS,)),
            dma((ROUNDS, 2)),
            *[dma((ROUNDS, 3))] * 2,
            *[dma((ROUNDS, 3))] * 2,
        ],
        compiler_params=pltpu.CompilerParams(
            collective_id=bit + 1, has_side_effects=True, vmem_limit_bytes=48 << 20
        ),
    )(*arrays)


def body(
    queries, new_keys, new_values, key_cache, value_cache, key_spill, value_spill,
    lengths, partner, out_weight,
):
    by_head = queries.reshape(ROWS, STEPS, GROUP, HEAD).transpose(0, 2, 1, 3)
    arrays = (
        lengths,
        by_head.reshape(ROUNDS, QB, HEAD),
        new_keys.reshape(ROUNDS, RB, HEAD),
        new_values.reshape(ROUNDS, RB, HEAD),
        *[a.reshape(ROWS, CAP, HEAD) for a in (key_cache, value_cache, key_spill, value_spill)],
        out_weight,
    )
    levels = lax.axis_size("dp").bit_length() - 1
    bit = 31 - lax.clz(partner[0])
    return lax.switch(bit, [functools.partial(attention, b) for b in range(levels)], *arrays)


def solution(mesh):
    return jax.shard_map(
        body,
        mesh=mesh,
        in_specs=(
            P("dp", None, "mp"),
            P("dp", None, "mp"),
            P("dp", None, "mp"),
            P("dp", "mp", None, None),
            P("dp", "mp", None, None),
            P("dp", "mp", None, None),
            P("dp", "mp", None, None),
            P(),
            P(),
            P("mp", "dp"),
        ),
        out_specs=P("mp", "dp"),
        check_vma=False,
    )
```

```python
import functools
import math

import jax
import jax.numpy as jnp
from jax import lax
from jax.experimental import pallas as pl
from jax.experimental.pallas import tpu as pltpu
from jax.sharding import PartitionSpec as P

MESH = pl.DeviceIdType.MESH
MASKED = -1e30
F32, BF16 = jnp.float32, jnp.bfloat16

ROWS = 16
STEPS = 4
GROUP = 12
HEAD = 128
CAP = 128
COLS = GROUP * HEAD
OUT_COLS = 384
ROUNDS = 4
RPR = ROWS // ROUNDS
RB = RPR * STEPS
QR = GROUP * STEPS
QB = RPR * QR
Z, X = 8, 4
PIECES = ((0, OUT_COLS), (OUT_COLS, 256), (OUT_COLS + 256, 128))
LAST = ROUNDS - 1
LAG = (1, 2, 2, 2, 2)
HANDED = ((0, OUT_COLS), (0, 256), (256, 128))
SCALE2 = math.log2(math.e) / math.sqrt(HEAD)


def kernel(
    bit,
    lengths_hbm, q_hbm, nk_hbm, nv_hbm, k_hbm, v_hbm, sk_hbm, sv_hbm, w_hbm,
    out,
    lengths, q_own, nk, nv, k, v, sk, sv, w, w_far, q_far, o_own, m_own, l_own,
    t_send, st_send, t_recv, st_recv, g, ps, px, py_send, py,
    load_sem, q_ss, q_rs, t_ss, t_rs, st_ss, st_rs, w_ss, w_rs, z_ss, z_rs, c_ss, c_rs,
    px_ss, px_rs, py_ss, py_rs,
):
    me, mp = lax.axis_index("dp"), lax.axis_index("mp")
    z, yh, c = me // 4, (me // 2) % 2, me % 2
    x, yl = mp // 2, mp % 2
    mask = 2**bit
    partner = me + mask * (1 - 2 * ((me // mask) % 2))

    def plane(d):
        return lax.rem(z + d + Z, Z)

    def along_z(d):
        return {"dp": plane(d) * 4 + yh * 2 + c, "mp": mp}

    def along_y(hi, lo):
        return {"dp": z * 4 + hi * 2 + c, "mp": x * 2 + lo}

    far = {"dp": partner, "mp": mp}
    sibling = {"dp": z * 4 + yh * 2 + 1 - c, "mp": mp}

    loads = [
        pltpu.make_async_copy(src, dst, load_sem.at[i])
        for i, (src, dst) in enumerate(
            [
                (q_hbm, q_own), (lengths_hbm, lengths), (nk_hbm, nk), (nv_hbm, nv), (k_hbm, k), (v_hbm, v),
                (sk_hbm, sk), (sv_hbm, sv), (w_hbm, w),
            ]
        )
    ]
    for load in loads:
        load.start()

    barrier = pltpu.get_barrier_semaphore()
    peers = [{"dp": me, "mp": lax.rem(x + j, X) * 2 + yl} for j in range(1, X)]
    column = [along_y(yh, 1 - yl), along_y(1 - yh, 0), along_y(1 - yh, 1)]
    greeted = [along_z(d) for d in (1, -1, 2, -2)] + [sibling, far] + column + peers
    for device in greeted:
        pl.semaphore_signal(barrier, inc=1, device_id=device, device_id_type=MESH)
    pl.semaphore_wait(barrier, len(greeted))

    def remote(src, dst, send_sem, recv_sem, device):
        return pltpu.make_async_remote_copy(
            src_ref=src, dst_ref=dst, send_sem=send_sem, recv_sem=recv_sem,
            device_id=device, device_id_type=MESH,
        )

    def q_copy(s):
        return remote(q_hbm.at[s], q_far.at[s], q_ss.at[s], q_rs.at[s], far)

    def t_copy(s):
        return remote(t_send.at[s], t_recv.at[s], t_ss.at[s], t_rs.at[s], far)

    def st_copy(s):
        return remote(st_send.at[s], st_recv.at[s], st_ss.at[s], st_rs.at[s], far)

    def w_copy(i):
        columns = pl.ds(256, 128) if i == 4 else pl.ds(0, 256)
        rows = pl.ds(0, COLS) if i == 4 else pl.ds(i * (COLS // 4), COLS // 4)
        return remote(
            w_hbm.at[rows, columns], w_far.at[rows, columns], w_ss.at[i], w_rs.at[i], along_y(1 - yh, yl)
        )

    for s in range(ROUNDS):
        q_copy(s).start()
    if bit != 1:
        for i in range(4):
            w_copy(i).start()
    for load in loads:
        load.wait()

    lane = lax.broadcasted_iota(jnp.int32, (1, CAP), 1)

    def bias_of(owner, s, less):
        return jnp.stack(
            [
                jnp.where(lane < lengths[owner * ROWS + s * RPR + r] - less, 0.0, MASKED)
                for r in range(RPR)
            ]
        )

    def scores_of(queries, keys, bias):
        raw = jnp.einsum("rqd,rkd->rqk", queries, keys, preferred_element_type=F32)
        return raw * SCALE2 + bias

    def own(s):
        q_row = lax.broadcasted_iota(jnp.int32, (QB, RB), 0)
        f_col = lax.broadcasted_iota(jnp.int32, (QB, RB), 1)
        first = (f_col >> 2) * QR
        fresh_ok = (q_row >= first) & (q_row < first + QR) & ((f_col & 3) <= (q_row & 3))
        fresh_bias = jnp.where(fresh_ok, 0.0, MASKED)
        rows = pl.ds(s * RPR, RPR)
        queries = q_own[s]
        cached = scores_of(queries.reshape(RPR, QR, HEAD), k[rows], bias_of(me, s, 0))
        fresh = lax.dot_general(
            queries, nk[s], (((1,), (1,)), ((), ())), preferred_element_type=F32
        )
        fresh = (fresh * SCALE2 + fresh_bias).reshape(RPR, QR, RB)
        peak = jnp.maximum(
            jnp.max(cached, axis=-1, keepdims=True), jnp.max(fresh, axis=-1, keepdims=True)
        )
        cached, fresh = jnp.exp2(cached - peak), jnp.exp2(fresh - peak)
        m_own[s] = peak
        l_own[s] = jnp.sum(cached, axis=-1, keepdims=True) + jnp.sum(fresh, axis=-1, keepdims=True)
        summed = jnp.einsum("rqk,rkd->rqd", cached.astype(BF16), v[rows], preferred_element_type=F32)
        o_own[s] = summed + jnp.dot(
            fresh.astype(BF16).reshape(QB, RB), nv[s], preferred_element_type=F32
        ).reshape(RPR, QR, HEAD)

    def diagonal():
        shape = (RPR, QR, CAP)
        return lax.broadcasted_iota(jnp.int32, shape, 1) == lax.broadcasted_iota(jnp.int32, shape, 2)

    def tail(s):
        rows = pl.ds(s * RPR, RPR)
        q_copy(s).wait_recv()
        scores = scores_of(q_far[s].reshape(RPR, QR, HEAD), sk[rows], bias_of(partner, s, CAP))
        peak = jnp.max(scores, axis=-1, keepdims=True)
        scores = jnp.exp2(scores - peak)
        weight = jnp.sum(scores, axis=-1, keepdims=True)
        summed = jnp.einsum("rqk,rkd->rqd", scores.astype(BF16), sv[rows], preferred_element_type=F32)
        t_send[s] = (summed / weight).astype(BF16).reshape(QB, HEAD)
        t_copy(s).start()
        st_send[s, 0:RPR] = jnp.sum(jnp.where(diagonal(), peak + jnp.log2(weight), 0.0), axis=1)
        st_copy(s).start()

        for i in range(ROUNDS):

            @pl.when(s == i)
            def _():
                if bit == 1:
                    w_copy(i).start()
                if i == ROUNDS - 1:
                    w_copy(4).start()

    def along(s, zz, d):
        ref = g.at[s, zz, c]
        return remote(ref, ref, z_ss.at[s], z_rs.at[s, zz], along_z(d))

    def to_core(s, zz, half):
        ref = g.at[s, zz, c]
        return remote(ref, ref, c_ss.at[s], c_rs.at[s, half], sibling)

    def merge(s):
        t_copy(s).wait_recv()
        st_copy(s).wait_recv()
        log_sum = jnp.sum(
            jnp.where(diagonal(), st_recv[s, 0:RPR][:, None, :], 0.0), axis=-1, keepdims=True
        )
        peak = jnp.maximum(m_own[s], log_sum)
        near_factor, far_factor = jnp.exp2(m_own[s] - peak), jnp.exp2(log_sum - peak)
        far_part = t_recv[s].reshape(RPR, QR, HEAD).astype(F32)
        total = near_factor * o_own[s] + far_factor * far_part
        context = (total / (near_factor * l_own[s] + far_factor)).astype(BF16)
        index = lax.broadcasted_iota(jnp.int32, (QB, QB), 0)
        source = ((index >> 2) & 3) * QR + (index >> 4) * STEPS + (index & 3)
        one_hot = jnp.where(lax.broadcasted_iota(jnp.int32, (QB, QB), 1) == source, 1.0, 0.0)
        heads = jnp.dot(
            one_hot.astype(BF16), context.reshape(QB, HEAD), preferred_element_type=F32
        ).astype(BF16)
        for h in range(GROUP):
            g[s, z, c, :, h * HEAD : (h + 1) * HEAD] = heads[h * RB : (h + 1) * RB]
        for d in (1, -1):
            along(s, z, d).start()

        to_core(s, z, 0).start()

    def ring(s, d):
        for zz, away in ((plane(-d), 1), (plane(d), -1)):
            along(s, zz, 1).wait_recv()
            if d < 3:
                along(s, zz, away).start()
            if d == 2:

                @pl.when(lax.rem(s, 2) == (1 - away) // 2)
                def _():
                    along(s, zz, 2 * away).start()

            to_core(s, zz, d // 3).start()
        if d == 3:
            along(s, plane(4), 1).wait_recv()
            to_core(s, plane(4), 1).start()

    def px_copy(s, j, i):
        columns = pl.ds(*PIECES[i])
        return remote(
            ps.at[s, pl.ds(2 * j, 2), :, columns], px.at[s, x, :, :, columns],
            px_ss.at[s, i], px_rs.at[s, i], {"dp": me, "mp": 2 * j + yl},
        )

    def px_arrived(s, i):
        ref = px.at[s, pl.ds(0, X - 1), :, :, pl.ds(*PIECES[i])]
        remote(ref, ref, px_ss.at[s, i], px_rs.at[s, i], sibling).wait_recv()

    def py_copy(s, k, i):
        device = along_y(1 - yh, k - 1) if k else along_y(yh, 1 - yl)
        columns = pl.ds(*HANDED[i])
        return remote(
            py_send.at[s, k, :, columns], py.at[s, 1 + yl if k else 0, :, columns],
            py_ss.at[s, i], py_rs.at[s, i], device,
        )

    def py_parts(ref, s, i):
        return ref.at[s, pl.ds(1, 2) if i else 0, :, pl.ds(*HANDED[i])]

    def project(s, weights, i):
        rows = g[s].reshape(Z * 2 * RB, COLS)
        start = PIECES[i][0]
        for weight in weights:
            product = jnp.dot(rows, weight, preferred_element_type=F32).astype(BF16)
            columns = slice(start, start + weight.shape[1])
            start += weight.shape[1]
            product = product.reshape(Z, 2 * RB, weight.shape[1])
            ps[s, :, :, columns] = product
            for j in range(X):

                @pl.when(x == j)
                def _():
                    px[s, j, :, :, columns] = product[2 * j : 2 * j + 2]

        for j in range(X):

            @pl.when(x != j)
            def _():
                px_copy(s, j, i).start()

    inner, outer = (0, -1, 1, -2, 2), (-3, 3, 4)

    def plane_copy(s, zz):
        columns = pl.ds(*PIECES[0])
        return remote(
            ps.at[s, zz, :, columns], px.at[s, x, lax.rem(zz, 2), :, columns],
            px_ss.at[s, 0], px_rs.at[s, 0], {"dp": me, "mp": (zz // 2) * 2 + yl},
        )

    def project_own(s, distances):
        half = int(distances == outer)
        ref = g.at[s, pl.ds(0, len(distances)), 1 - c]
        remote(ref, ref, c_ss.at[s], c_rs.at[s, half], sibling).wait_recv()
        planes = [plane(d) for d in distances]
        rows = jnp.concatenate([g[s, zz].reshape(2 * RB, COLS) for zz in planes], axis=0)
        product = jnp.dot(rows, w[...], preferred_element_type=F32).astype(BF16)
        for j, zz in enumerate(planes):
            mine = product[j * 2 * RB : (j + 1) * 2 * RB]

            @pl.when(zz // 2 != x)
            def _():
                ps[s, zz, :, :OUT_COLS] = mine
                plane_copy(s, zz).start()

            @pl.when(zz // 2 == x)
            def _():
                px[s, x, lax.rem(zz, 2), :, :OUT_COLS] = mine

    def project_first(s):
        @pl.when(s == 0)
        def _():
            for i in range(4):
                w_copy(i).wait_recv()

        project(s, (w_far[:, :256],), 1)

    def project_second(s):
        @pl.when(s == 0)
        def _():
            w_copy(4).wait_recv()

        project(s, (w_far[:, 256:],), 2)

    def sum_x(s, lo, columns):
        total = px[s, 0, lo, :, columns].astype(F32)
        for j in range(1, X):
            total = total + px[s, j, lo, :, columns].astype(F32)
        return total

    def hand_over(s, i):
        start, size = HANDED[i]
        offset = OUT_COLS if i else 0
        for k in (1, 2) if i else (0,):
            total = sum_x(s, k - 1 if k else 1 - yl, slice(offset + start, offset + start + size))
            py_send[s, k, :, start : start + size] = total.astype(BF16)
            py_copy(s, k, i).start()

    def hand_first(s):
        px_arrived(s, 0)
        hand_over(s, 0)
        px_arrived(s, 1)
        hand_over(s, 1)

    def hand_second(s):
        px_arrived(s, 2)
        hand_over(s, 2)

    def finish(s):
        for i in range(3):
            ref = py_parts(py, s, i)
            remote(ref, ref, py_ss.at[s, i], py_rs.at[s, i], sibling).wait_recv()
        own_rows = sum_x(s, yl, slice(0, OUT_COLS)) + py[s, 0].astype(F32)
        far_rows = py[s, 1].astype(F32) + py[s, 2].astype(F32)
        for hi, total in ((yh, own_rows), (1 - yh, far_rows)):
            for i in range(2):
                start = (hi * 2 + i) * ROWS * STEPS + s * RB
                part = total[i * RB : (i + 1) * RB].astype(BF16)
                out[pl.ds(pl.multiple_of(start, RB), RB), :] = part

    part, early = functools.partial, bit >= 3
    stages = [(own, (0, 1, 2, 3)), (tail, (0, 1, 2, 3))] + [
        (stage, tuple(at + LAG[bit] for at in slots))
        for stage, slots in (
            (merge, (0, 1, 2, 3)),
            (part(ring, d=1), (1, 2, 3, 4)),
            (part(ring, d=2), (2, 3, 4, 5)),
            (part(ring, d=3), (3, 4, 5, 6)),
            (part(project_own, distances=outer), (4, 5, 6, 6)),
            (part(project_own, distances=inner), (3, 4, 5, 5)),
            (project_first, (4, 5, 6, 6)),
            (hand_first, (6, 6, 7, 7)),
            (project_second, (5, 5, 6, 6) if early else (5, 6, 6, 6) if bit == 2 else (6, 6, 6, 6)),
            (hand_second, (6, 7, 7, 7) if early else (7, 7, 7, 7)),
            (finish, (8, 8, 8, 8)),
        )
    ]

    def slot(t, carry):
        for stage, slots in stages:

            def one(s, inside, stage=stage):
                stage(s)
                return inside

            begun = sum((t > at).astype(jnp.int32) for at in slots)
            due = sum((t >= at).astype(jnp.int32) for at in slots)
            lax.fori_loop(begun, due, one, 0)

        return carry

    lax.fori_loop(0, 1 + max(slots[-1] for _, slots in stages), slot, 0)

    def drain(s, carry):
        q_copy(s).wait_send()
        t_copy(s).wait_send()
        st_copy(s).wait_send()
        for ref, sem in (
            (g.at[s, pl.ds(0, 7), 0], z_ss.at[s]),
            (g.at[s, :, 0], c_ss.at[s]),
            *[(ps.at[s, pl.ds(0, 2 * X - 2), :, pl.ds(*PIECES[i])], px_ss.at[s, i]) for i in range(3)],
            *[(py_parts(py_send, s, i), py_ss.at[s, i]) for i in range(3)],
        ):
            remote(ref, ref, sem, c_rs.at[s, 0], sibling).wait_send()
        return carry

    lax.fori_loop(0, ROUNDS, drain, 0)
    for i in range(5):
        w_copy(i).wait_send()


def attention(bit, *arrays):
    any_space = pl.BlockSpec(memory_space=pl.ANY)
    dma = pltpu.SemaphoreType.DMA
    return pl.pallas_call(
        functools.partial(kernel, bit),
        name=f"attention_{bit}",
        out_shape=jax.ShapeDtypeStruct((4 * ROWS * STEPS, OUT_COLS), BF16),
        in_specs=[any_space] * 9,
        out_specs=pl.BlockSpec(memory_space=pltpu.VMEM),
        scratch_shapes=[
            pltpu.SMEM((ROWS * 32,), jnp.int32),
            pltpu.VMEM((ROUNDS, QB, HEAD), BF16),
            *[pltpu.VMEM((ROUNDS, RB, HEAD), BF16)] * 2,
            *[pltpu.VMEM((ROWS, CAP, HEAD), BF16)] * 4,
            *[pltpu.VMEM((COLS, OUT_COLS), BF16)] * 2,
            pltpu.VMEM((ROUNDS, QB, HEAD), BF16),
            pltpu.VMEM((ROUNDS, RPR, QR, HEAD), F32),
            pltpu.VMEM((ROUNDS, RPR, QR, 1), F32),
            pltpu.VMEM((ROUNDS, RPR, QR, 1), F32),
            pltpu.VMEM((ROUNDS, QB, HEAD), BF16),
            pltpu.VMEM((ROUNDS, 8, HEAD), F32),
            pltpu.VMEM((ROUNDS, QB, HEAD), BF16),
            pltpu.VMEM((ROUNDS, 8, HEAD), F32),
            pltpu.VMEM((ROUNDS, Z, 2, RB, COLS), BF16),
            pltpu.VMEM((ROUNDS, Z, 2 * RB, 2 * OUT_COLS), BF16),
            pltpu.VMEM((ROUNDS, X, 2, 2 * RB, 2 * OUT_COLS), BF16),
            pltpu.VMEM((ROUNDS, 3, 2 * RB, OUT_COLS), BF16),
            pltpu.VMEM((ROUNDS, 3, 2 * RB, OUT_COLS), BF16),
            dma((9,)),
            *[dma((ROUNDS,))] * 6,
            *[dma((5,))] * 2,
            dma((ROUNDS,)),
            dma((ROUNDS, Z)),
            dma((ROUNDS,)),
            dma((ROUNDS, 2)),
            *[dma((ROUNDS, 3))] * 2,
            *[dma((ROUNDS, 3))] * 2,
        ],
        compiler_params=pltpu.CompilerParams(
            collective_id=bit + 1, has_side_effects=True, vmem_limit_bytes=48 << 20
        ),
    )(*arrays)


def body(
    queries, new_keys, new_values, key_cache, value_cache, key_spill, value_spill,
    lengths, partner, out_weight,
):
    by_head = queries.reshape(ROWS, STEPS, GROUP, HEAD).transpose(0, 2, 1, 3)
    arrays = (
        lengths,
        by_head.reshape(ROUNDS, QB, HEAD),
        new_keys.reshape(ROUNDS, RB, HEAD),
        new_values.reshape(ROUNDS, RB, HEAD),
        *[a.reshape(ROWS, CAP, HEAD) for a in (key_cache, value_cache, key_spill, value_spill)],
        out_weight,
    )
    levels = lax.axis_size("dp").bit_length() - 1
    bit = 31 - lax.clz(partner[0])
    return lax.switch(bit, [functools.partial(attention, b) for b in range(levels)], *arrays)


def solution(mesh):
    return jax.shard_map(
        body,
        mesh=mesh,
        in_specs=(
            P("dp", None, "mp"),
            P("dp", None, "mp"),
            P("dp", None, "mp"),
            P("dp", "mp", None, None),
            P("dp", "mp", None, None),
            P("dp", "mp", None, None),
            P("dp", "mp", None, None),
            P(),
            P(),
            P("mp", "dp"),
        ),
        out_specs=P("mp", "dp"),
        check_vma=False,
    )
```
